32 devices in a mesh: space: 4 (over z), sample: 8 (over y, x, core).
Axes of the slice: x: 2, y: 2, z: 4, core: 2. Of those that a mesh axis runs over, the one named last changes fastest.
Arguments:
- mean_field: float32 [4, 48, 128], P('space'), may hold values from -0.6 to 0.6
- modes: bfloat16 [64, 4, 48, 128], P(None, 'space'), may hold values from -6 to 6
- coeffs: bfloat16 [64, 3072], P(None, 'sample'), may hold values from -6 to 6
- kicks: float32 [64, 3072], P(None, 'sample'), may hold values from -6 to 6
Outputs:
- new_mean: float32 [4, 48, 128], P('space')
- new_modes: float32 [64, 4, 48, 128], P(None, 'space')
- new_coeffs: float32 [64, 3072], P(None, 'sample')
The draws below stay inside these ranges and needn't reach their ends.
All inputs are finite; a program needn't handle non-finite values.
Results may differ from the reference program's by a relative error of at most 0.0023.
Values may be sent and summed in bfloat16 or wider, within the bound.
A program may use at most 64 MiB of HBM per device.

```python
import jax
import jax.numpy as jnp
from jax import lax

RANK = 64
GY = 48
GZ = 128
NX = 4
CELLS = 24576
SAMPLES = 3072


def shard_levels(rng, extent, cuts, low, largest):
    gain = 1.0
    for dim, parts in cuts:
        steps = jax.random.uniform(jax.random.fold_in(jax.random.fold_in(rng, 6), dim), (parts,), jnp.float32, low / len(cuts), largest / len(cuts))
        gain = gain * jnp.repeat(jnp.exp(steps), extent[dim] // parts).reshape((-1,) + (1,) * (len(extent) - 1 - dim))
    return gain


def noise(key, extent, width, most, cuts=(), kind=jnp.bfloat16):
    entries = width * jax.random.normal(key, extent, jnp.float32)
    if cuts:
        entries = entries * shard_levels(key, extent, cuts, -0.22, 0.18)
    return jnp.clip(entries, -most, most).astype(kind)


def setup_inputs(seed: int = 0) -> dict:
    streams_of = jax.random.split(jax.random.key(seed), 5)
    mean_field = jnp.clip(jax.random.uniform(streams_of[0], (NX, GY, GZ), jnp.float32, -0.6, 0.6) * shard_levels(streams_of[0], (NX, GY, GZ), ((0, 4),), -0.4, 0.0), -0.6, 0.6)
    modes = noise(streams_of[1], (RANK, NX, GY, GZ), 1.0, 6.0, ((1, 4),))
    coeffs = noise(streams_of[2], (RANK, SAMPLES), 1.0, 6.0, ((1, 8),))
    kicks = noise(streams_of[3], (RANK, SAMPLES), 1.0, 6.0, ((1, 8),), jnp.float32)
    return {"mean_field": mean_field, "modes": modes, "coeffs": coeffs, "kicks": kicks}


amplitude = 0.1
reaction = 2.0
diffusion = 0.25
time_step = 0.1
noise_level = 0.3

def laplace(values):
    pads = [(0, 0)] * (values.ndim - 3) + [(1, 1)] * 3
    padded = jnp.pad(values, pads)
    neighbours = padded[..., 2:, 1:-1, 1:-1] + padded[..., :-2, 1:-1, 1:-1]
    neighbours = neighbours + padded[..., 1:-1, 2:, 1:-1] + padded[..., 1:-1, :-2, 1:-1]
    neighbours = neighbours + padded[..., 1:-1, 1:-1, 2:] + padded[..., 1:-1, 1:-1, :-2]
    return neighbours - 6.0 * values

def reference(mean_field, modes, coeffs, kicks):
    high = lax.Precision.HIGHEST
    modes_f = modes.astype(jnp.float32)
    coeff_f = coeffs.astype(jnp.float32)
    lap_modes = laplace(modes_f)
    lap_mean = laplace(mean_field)

    def plane_terms(position):
        plane_modes = lax.dynamic_index_in_dim(modes_f, position, 1, keepdims=False).reshape(RANK, GY * GZ)
        plane_mean = lax.dynamic_index_in_dim(mean_field, position, 0, keepdims=False).reshape(GY * GZ)
        total = plane_mean[None, :] + amplitude * jnp.dot(coeff_f.T, plane_modes, precision=high)
        react = (reaction * (total - total * total * total)).astype(jnp.bfloat16)
        react = lax.optimization_barrier(react).astype(jnp.float32)
        mode_part = jnp.dot(coeff_f, react, precision=high)
        coef_part = jnp.dot(plane_modes, react.T, precision=high)
        return (mode_part, coef_part, jnp.sum(react, axis=0))
    mode_parts, coef_parts, react_parts = lax.map(plane_terms, jnp.arange(NX, dtype=jnp.int32))
    mode_force = jnp.transpose(mode_parts, (1, 0, 2)).reshape(RANK, CELLS)
    coef_force = jnp.sum(coef_parts, axis=0)
    react_mean = react_parts.reshape(CELLS) / SAMPLES
    covariance = jnp.dot(coeff_f, coeff_f.T, precision=high) / SAMPLES
    chol = jnp.linalg.cholesky(covariance)
    flat_modes = modes_f.reshape(RANK, CELLS)
    flat_lap = lap_modes.reshape(RANK, CELLS)
    drive = jax.scipy.linalg.cho_solve((chol, True), mode_force / (amplitude * SAMPLES)) + diffusion * flat_lap
    stiff = jnp.dot(flat_modes, flat_lap.T, precision=high) / CELLS
    correlation = jnp.dot(flat_modes, drive.T, precision=high) / CELLS
    shift = jnp.dot(flat_modes, react_mean, precision=high)
    new_mean = mean_field + time_step * (diffusion * lap_mean + react_mean.reshape(NX, GY, GZ))
    moved = drive - jnp.dot(correlation.T, flat_modes, precision=high)
    new_modes = (flat_modes + time_step * moved).reshape(RANK, NX, GY, GZ)
    rate = (coef_force - shift[:, None]) / (amplitude * CELLS) + diffusion * jnp.dot(stiff, coeff_f, precision=high)
    new_coeffs = coeff_f + time_step * rate + noise_level * time_step ** 0.5 * kicks
    return (new_mean, new_modes, new_coeffs)
```

```python
import functools

import jax
import jax.numpy as jnp
from jax import lax
from jax.experimental import pallas as pl
from jax.experimental.pallas import tpu as pltpu
from jax.sharding import PartitionSpec as P

MESH = pl.DeviceIdType.MESH
F32 = jnp.float32
BF16 = jnp.bfloat16
HIGH = lax.Precision.HIGHEST

amplitude = 0.1
reaction = 2.0
diffusion = 0.25
time_step = 0.1
noise_level = 0.3


def dot_nt(a, b, precision=None):
    return lax.dot_general(
        a, b, (((1,), (1,)), ((), ())), precision=precision, preferred_element_type=F32
    )


def dot_nn(a, b, precision=None):
    return jnp.dot(a, b, precision=precision, preferred_element_type=F32)


def rows_of(parts, shape):
    row = lax.broadcasted_iota(jnp.int32, shape, 0)
    block = jnp.zeros(shape, F32)
    for i, part in enumerate(parts):
        block = jnp.where(row == i, part, block)
    return block


def split(value):
    high = value.astype(BF16).astype(F32)
    return high, value - high


def invert(a):
    n = a.shape[0]
    lane = lax.broadcasted_iota(jnp.int32, (1, a.shape[1]), 1)
    row_id = lax.broadcasted_iota(jnp.int32, (n, 1), 0)
    for k in range(n):
        col = a[:, k : k + 1]
        row = a[k : k + 1, :]
        pivot = 1.0 / row[:, k : k + 1]
        row = jnp.where(lane == k, 1.0, row) * pivot
        a = jnp.where(lane == k, 0.0, a) - col * row
        a = jnp.where(row_id == k, row, a)
    return a


def kernel(
    nz, ns, blk, gz,
    mean_ref, modes_ref, coeffs_ref, kicks_ref,
    mean_out, modes_out, coeffs_out,
    maug, caug, ctaug, before, after, rbuf, gacc, fsend, frecv, gath,
    m1s, m1z, m2s, m2z, gbuf,
    h_ss, h_rs, f_ss, f_rs, u_ss, u_rs, g_ss, g_rs,
    a_ss, a_rs, b_ss, b_rs, c_ss, c_rs, d_ss, d_rs,
):
    z = lax.axis_index("space")
    s = lax.axis_index("sample")
    rank, cells = modes_ref.shape
    samples = coeffs_ref.shape[1]
    aug = maug.shape[0]
    total_cells = cells * nz
    total_samples = samples * ns

    barrier = pltpu.get_barrier_semaphore()
    for k in range(1, ns):
        pl.semaphore_signal(
            barrier, inc=1, device_id={"sample": lax.rem(s + k, ns)}, device_id_type=MESH
        )
    for k in range(1, nz):
        pl.semaphore_signal(
            barrier, inc=1, device_id={"space": lax.rem(z + k, nz)}, device_id_type=MESH
        )

    def peer_copy(src, dst, send, recv, axis, me, n, k):
        return pltpu.make_async_remote_copy(
            src_ref=src,
            dst_ref=dst.at[k],
            send_sem=send.at[k - 1],
            recv_sem=recv.at[k - 1],
            device_id={axis: lax.rem(me + k, n)},
            device_id_type=MESH,
        )

    def send_all(buf, send, recv, axis, me, n):
        for k in range(1, n):
            peer_copy(buf.at[0], buf, send, recv, axis, me, n, k).start()

    def sum_all(buf, send, recv, axis, me, n):
        for k in range(1, n):
            peer_copy(buf.at[0], buf, send, recv, axis, me, n, k).wait_recv()
        total = buf[me].astype(F32)
        for j in range(1, n):
            total = total + buf[lax.rem(me - j + n, n)].astype(F32)
        return total

    def drain(buf, send, recv, axis, me, n):
        for k in range(1, n):
            peer_copy(buf.at[0], buf, send, recv, axis, me, n, k).wait_send()

    maug[:, :gz] = jnp.zeros((aug, gz), BF16)
    maug[:, gz + cells :] = jnp.zeros((aug, gz), BF16)
    maug[:rank, gz : gz + cells] = modes_ref[...]
    mean = mean_ref[...]
    hi, rest = split(mean)
    mid, low = split(rest)
    maug[rank:, gz : gz + cells] = rows_of((hi, mid, low), (aug - rank, cells)).astype(BF16)

    pl.semaphore_wait(barrier, ns + nz - 2)

    own = pl.multiple_of(s * blk, blk)
    halo = maug.at[:, pl.ds(pl.multiple_of(own + gz, gz), blk)]
    to_up = pltpu.make_async_remote_copy(
        src_ref=halo, dst_ref=before, send_sem=h_ss.at[0], recv_sem=h_rs.at[0],
        device_id={"space": lax.rem(z + 1, nz)}, device_id_type=MESH,
    )
    to_down = pltpu.make_async_remote_copy(
        src_ref=halo, dst_ref=after, send_sem=h_ss.at[1], recv_sem=h_rs.at[1],
        device_id={"space": lax.rem(z + nz - 1, nz)}, device_id_type=MESH,
    )

    @pl.when(z < nz - 1)
    def _():
        to_up.start()

    @pl.when(z > 0)
    def _():
        to_down.start()

    coeff_f = coeffs_ref[...].astype(F32)
    pad = jnp.where(
        lax.broadcasted_iota(jnp.int32, (caug.shape[0] - rank, samples), 0) < 3, 10.0, 0.0
    )
    full = jnp.concatenate([coeff_f, pad], axis=0)
    caug[...] = full.astype(BF16)
    ctaug[...] = full.T.astype(BF16)
    gacc[...] = jnp.zeros_like(gacc)

    sub = 256 if blk % 256 == 0 else 128

    def block(k, carry):
        owner = lax.rem(s + k, ns)
        base = pl.multiple_of(owner * blk, blk)
        for j in range(blk // sub):
            at = pl.multiple_of(base + (gz + j * sub), 128)
            u = amplitude * dot_nn(ctaug[:, :aug], maug[:, pl.ds(at, sub)])
            r = (reaction * (u - u * u * u)).astype(BF16)
            rbuf[:, j * sub : (j + 1) * sub] = r
        r = rbuf[...]
        f = dot_nn(caug[:aug, :], r)
        gacc[...] += dot_nt(maug[:rank, pl.ds(pl.multiple_of(base + gz, 128), blk)], r)
        fsend[k] = f[: rank + 8]

        @pl.when(k < ns)
        def _():
            pltpu.make_async_remote_copy(
                src_ref=fsend.at[k], dst_ref=frecv.at[k],
                send_sem=f_ss.at[k - 1], recv_sem=f_rs.at[k - 1],
                device_id={"sample": owner}, device_id_type=MESH,
            ).start()

        return carry

    first = ns // 4
    lax.fori_loop(1, 1 + first, block, 0)

    @pl.when(z > 0)
    def _():
        to_up.wait_recv()

    @pl.when(z == 0)
    def _():
        before[...] = jnp.zeros_like(before)

    @pl.when(z < nz - 1)
    def _():
        to_down.wait_recv()

    @pl.when(z == nz - 1)
    def _():
        after[...] = jnp.zeros_like(after)

    gap = jnp.abs(
        lax.broadcasted_iota(jnp.int32, (gz, gz), 0) - lax.broadcasted_iota(jnp.int32, (gz, gz), 1)
    )
    line = jnp.where(gap == 0, -6.0, jnp.where(gap == 1, 1.0, 0.0)).astype(BF16)

    def laplace():
        parts = []
        for j in range(blk // gz):
            at = own + (gz + j * gz)
            centre = maug[:, pl.ds(pl.multiple_of(at, gz), gz)]
            part = dot_nn(centre, line)
            for d in (-gz, gz):
                part = part + maug[:, pl.ds(pl.multiple_of(at + d, gz), gz)].astype(F32)
            part = part + before[:, j * gz : (j + 1) * gz].astype(F32)
            part = part + after[:, j * gz : (j + 1) * gz].astype(F32)
            parts.append(part)
        return jnp.concatenate(parts, axis=1)

    lap = laplace()
    own_modes = maug[:rank, pl.ds(pl.multiple_of(own + gz, 128), blk)]
    lap_hi, lap_lo = split(lap[:rank])
    zero_blk = jnp.zeros((rank, blk), BF16)
    packed = dot_nt(own_modes, jnp.concatenate([zero_blk, lap_hi.astype(BF16)], axis=0))
    packed += dot_nt(own_modes, jnp.concatenate([zero_blk, lap_lo.astype(BF16)], axis=0))
    coeffs = coeffs_ref[...]
    packed += dot_nt(coeffs, jnp.concatenate([coeffs, jnp.zeros_like(coeffs)], axis=0))
    m1s[0] = packed
    st1 = (m1s, a_ss, a_rs, "sample", s, ns)
    send_all(*st1)

    second = ns // 2
    lax.fori_loop(1 + first, 1 + second, block, 0)
    m1z[0] = sum_all(*st1)
    st2 = (m1z, b_ss, b_rs, "space", z, nz)
    send_all(*st2)
    lax.fori_loop(1 + second, 1 + ns, block, 0)

    g = gacc[...]
    m2s[0] = dot_nt(g, caug[...].astype(F32), HIGH)
    st3 = (m2s, c_ss, c_rs, "sample", s, ns)
    send_all(*st3)
    gbuf[0] = g

    m1_sum = sum_all(*st2)
    cov = jnp.where(
        lax.broadcasted_iota(jnp.int32, (rank, 2 * rank), 1) < rank, m1_sum, 0.0
    ) * (1.0 / (nz * total_samples))
    inverse = invert(cov)
    stiff = pltpu.roll(m1_sum, rank, 1)[:, :rank] * (1.0 / total_cells)

    m2z[0] = sum_all(*st3)
    st4 = (m2z, d_ss, d_rs, "space", z, nz)
    send_all(*st4)
    st5 = (gbuf, g_ss, g_rs, "space", z, nz)
    send_all(*st5)

    force = fsend[ns]
    for k in range(1, ns):
        peer_copy(fsend.at[k], frecv, f_ss, f_rs, "sample", s, ns, k).wait_recv()
        force = force + frecv[k]
    solved = dot_nn(inverse[:, :rank], force[:rank], HIGH) * (1.0 / total_samples)
    partial = solved + (time_step * diffusion) * lap[:rank]
    react_mean = force[rank : rank + 1] * (1.0 / (10.0 * total_samples))
    lap_mean = lap[rank : rank + 1] + lap[rank + 1 : rank + 2] + lap[rank + 2 : rank + 3]
    mean_upd = time_step * (diffusion * lap_mean + react_mean)
    gath[0, rank:, :] = rows_of(split(mean_upd), (aug - rank, blk)).astype(BF16)

    m2_sum = sum_all(*st4)
    weights = dot_nt(inverse, m2_sum, HIGH) * (1.0 / (float(total_samples) * total_cells))
    weights = weights + (time_step * diffusion) * stiff
    update = partial - dot_nn(weights, own_modes.astype(F32), HIGH)
    gath[0, :rank, :] = update.astype(BF16)
    st6 = (gath, u_ss, u_rs, "sample", s, ns)
    send_all(*st6)

    coef_force = sum_all(*st5)
    shift = m2_sum[:, rank : rank + 1] * (1.0 / (10.0 * total_samples))
    coeff_f = coeffs_ref[...].astype(F32)
    rate = (coef_force - shift) * (1.0 / (amplitude * total_cells))
    rate = rate + diffusion * dot_nn(stiff, coeff_f, HIGH)
    coeffs_out[...] = coeff_f + time_step * rate + (noise_level * time_step**0.5) * kicks_ref[...]

    def finish(k):
        base = pl.multiple_of(lax.rem(s - k + ns, ns) * blk, blk)
        cols = pl.ds(base, blk)
        old = maug[:rank, pl.ds(pl.multiple_of(base + gz, 128), blk)].astype(F32)
        modes_out[:, cols] = old + gath[k, :rank, :].astype(F32)
        tail = gath[k, rank:, :].astype(F32)
        mean_out[:, cols] = mean_ref[:, cols] + (tail[0:1] + tail[1:2])

    finish(0)
    for k in range(1, ns):
        peer_copy(gath.at[0], gath, u_ss, u_rs, "sample", s, ns, k).wait_recv()
        finish(k)

    for stage in (st1, st2, st3, st4, st5, st6):
        drain(*stage)
    for k in range(1, ns):
        peer_copy(fsend.at[k], frecv, f_ss, f_rs, "sample", s, ns, k).wait_send()

    @pl.when(z < nz - 1)
    def _():
        to_up.wait_send()

    @pl.when(z > 0)
    def _():
        to_down.wait_send()


def per_device(nz, ns, mean_field, modes, coeffs, kicks):
    rank, planes, gy, gz = modes.shape
    cells = planes * gy * gz
    samples = coeffs.shape[1]
    blk = cells // ns
    aug = rank + 16
    wide = 2 * rank
    dma = pltpu.SemaphoreType.DMA
    vm = pltpu.VMEM
    scratch = [
        vm((aug, cells + 2 * gz), BF16),
        vm((wide, samples), BF16),
        vm((samples, wide), BF16),
        vm((aug, blk), BF16),
        vm((aug, blk), BF16),
        vm((samples, blk), BF16),
        vm((rank, samples), F32),
        vm((ns + 1, rank + 8, blk), F32),
        vm((ns, rank + 8, blk), F32),
        vm((ns, aug, blk), BF16),
        vm((ns, rank, wide), F32),
        vm((nz, rank, wide), F32),
        vm((ns, rank, wide), F32),
        vm((nz, rank, wide), F32),
        vm((nz, rank, samples), F32),
    ]
    scratch += [dma((2,)), dma((2,))]
    for n in (ns, ns, nz, ns, nz, ns, nz):
        scratch += [dma((n - 1,)), dma((n - 1,))]
    spec = pl.BlockSpec(memory_space=pltpu.VMEM)
    out = pl.pallas_call(
        functools.partial(kernel, nz, ns, blk, gz),
        out_shape=(
            jax.ShapeDtypeStruct((1, cells), F32),
            jax.ShapeDtypeStruct((rank, cells), F32),
            jax.ShapeDtypeStruct((rank, samples), F32),
        ),
        in_specs=[spec] * 4,
        out_specs=(spec,) * 3,
        scratch_shapes=scratch,
        compiler_params=pltpu.CompilerParams(
            collective_id=0, has_side_effects=True, vmem_limit_bytes=40 * 2**20
        ),
        name="step",
    )(mean_field.reshape(1, cells), modes.reshape(rank, cells), coeffs, kicks)
    new_mean, new_modes, new_coeffs = out
    return (
        new_mean.reshape(planes, gy, gz),
        new_modes.reshape(rank, planes, gy, gz),
        new_coeffs,
    )


def solution(mesh):
    nz, ns = mesh.shape["space"], mesh.shape["sample"]
    return jax.shard_map(
        functools.partial(per_device, nz, ns),
        mesh=mesh,
        in_specs=(
            P("space", None, None),
            P(None, "space", None, None),
            P(None, "sample"),
            P(None, "sample"),
        ),
        out_specs=(P("space", None, None), P(None, "space", None, None), P(None, "sample")),
        check_vma=False,
    )
```
